32 devices in a mesh: section: 2 (over core), dp: 16 (over z, y, x).
Axes of the slice: x: 2, y: 2, z: 4, core: 2. Of those that a mesh axis runs over, the one named last changes fastest.
Arguments:
- tokens: bfloat16 [16384, 1088], P('dp'), may hold values from -6 to 6
- positions: int32 [16384], P('dp'), may hold values from 0 to 511, as said below
- cotangent: bfloat16 [16384, 1088], P('dp'), may hold values from -6 to 6
- w_qkv: bfloat16 [2, 1088, 3264], P('section', 'dp'), may hold values from -0.1875 to 0.1875
- w_out: bfloat16 [2, 1088, 1088], P('section', 'dp'), may hold values from -1 to 1
- w_up: bfloat16 [2, 1088, 4352], P('section', 'dp'), may hold values from -0.1875 to 0.1875
- w_down: bfloat16 [2, 4352, 1088], P('section', 'dp'), may hold values from -0.09375 to 0.09375
- norm_gains: bfloat16 [2, 2, 1088], P('section', None, 'dp'), may hold values from 0.5 to 1.5
- biases: bfloat16 [2, 6, 1088], P('section', None, 'dp'), may hold values from -3 to 3
- up_bias: bfloat16 [2, 4352], P('section', 'dp'), may hold values from -3 to 3
Outputs:
- section_acts: bfloat16 [2, 16384, 1088], P('section', 'dp')
- section_grads: float32 [2, 16384, 1088], P('section', 'dp')
- grad_qkv: float32 [2, 1088, 3264], P('section', 'dp')
- grad_out: float32 [2, 1088, 1088], P('section', 'dp')
- grad_up: float32 [2, 1088, 4352], P('section', 'dp')
- grad_down: float32 [2, 4352, 1088], P('section', 'dp')
- grad_gains: float32 [2, 2, 1088], P('section', None, 'dp')
- grad_biases: float32 [2, 6, 1088], P('section', None, 'dp')
- grad_up_bias: float32 [2, 4352], P('section', 'dp')
The draws below stay inside these ranges and needn't reach their ends.
Inputs may be any that keep to these rules, and one draw needn't show every extreme that they name: positions[i] is 0 where a sequence starts and positions[i - 1] + 1 elsewhere; every aligned block of 512 tokens starts a sequence, so no sequence crosses such a block; some block holds a single sequence of 512 tokens.
All inputs are finite; a program needn't handle non-finite values.
Results may differ from the reference program's by a relative error of at most 0.014.
Values may be sent and summed in bfloat16 or wider, within the bound.
No kernel may reach another device: no remote copies, remote signals or barrier semaphores. Data moves between devices by JAX's collectives and lax.ppermute only.
A program may use at most 576 MiB of HBM per device.

```python
import jax
import jax.numpy as jnp
from jax import lax

D = 1088
HEADS = 17
HEAD_DIM = 64
FF = 4352
SEQ = 512
TOKENS = 16384


def draw_positions(key, part):
    key = jax.random.fold_in(key, 11)
    block_count = TOKENS // SEQ
    pick_key, level_key, cut_key = jax.random.split(key, 3)
    levels = jax.random.randint(level_key, (block_count, 1), 1, 10)
    raw_bits = jax.random.randint(cut_key, (block_count, SEQ), 0, 1 << 20)
    threshold = jnp.right_shift(jnp.int32(1 << 20), levels)
    cuts = raw_bits < threshold
    whole_block = jax.random.randint(pick_key, (), 0, block_count)
    index_row = jnp.arange(SEQ, dtype=jnp.int32)[None, :]
    block_ids = jnp.arange(block_count, dtype=jnp.int32)[:, None]
    cuts = cuts & (block_ids != whole_block) | (index_row == 0)
    starts = lax.cummax(jnp.where(cuts, index_row, 0), axis=1)
    return (index_row - starts).reshape(TOKENS).astype(jnp.int32)


def block_levels(rng, extent, cuts, low, top_value):
    gain = 1.0
    for dim, shards_of in cuts:
        steps = jax.random.uniform(jax.random.fold_in(jax.random.fold_in(rng, 6), dim), (shards_of,), jnp.float32, low / len(cuts), top_value / len(cuts))
        gain = gain * jnp.repeat(jnp.exp(steps), extent[dim] // shards_of).reshape((-1,) + (1,) * (len(extent) - 1 - dim))
    return gain


def normal_values(own_key, shape, width, limit, shards=(), kind=jnp.bfloat16):
    result = width * jax.random.normal(own_key, shape, jnp.float32)
    if shards:
        result = result * block_levels(own_key, shape, shards, -0.22, 0.18)
    return jnp.clip(result, -limit, limit).astype(kind)


def setup_inputs(seed: int = 0) -> dict:
    splits = jax.random.split(jax.random.key(seed), 11)
    tokens = normal_values(splits[0], (TOKENS, D), 1.0, 6.0, ((0, 16),))
    positions = draw_positions(jax.random.fold_in(splits[10], 71), 0)
    cotangent = normal_values(splits[2], (TOKENS, D), 1.0, 6.0, ((0, 16),))
    w_qkv = normal_values(splits[3], (2, D, 3 * D), D ** -0.5, 0.1875, ((0, 2), (1, 16)))
    w_out = normal_values(splits[4], (2, D, D), (D // 32) ** -0.5, 1.0, ((0, 2), (1, 16)))
    w_up = normal_values(splits[5], (2, D, FF), D ** -0.5, 0.1875, ((0, 2), (1, 16)))
    w_down = normal_values(splits[6], (2, FF, D), FF ** -0.5, 0.09375, ((0, 2), (1, 16)))
    norm_gains = jnp.clip(1.0 + 0.1 * jax.random.normal(splits[7], (2, 2, D), jnp.float32), 0.5, 1.5).astype(jnp.bfloat16)
    biases = normal_values(splits[8], (2, 6, D), 0.5, 3.0, ((0, 2), (2, 16)))
    up_bias = normal_values(splits[9], (2, FF), 0.5, 3.0, ((0, 2), (1, 16)))
    return {"tokens": tokens, "positions": positions, "cotangent": cotangent, "w_qkv": w_qkv, "w_out": w_out, "w_up": w_up, "w_down": w_down, "norm_gains": norm_gains, "biases": biases, "up_bias": up_bias}


EPSILON = 1e-05

@jax.custom_vjp
def low(v):
    return lax.optimization_barrier(v.astype(jnp.bfloat16)).astype(jnp.float32)

@jax.custom_vjp
def low_back(v):
    return v

def low_keep(v):
    return (low(v), None)

def low_pass(kept, grad):
    return (grad,)

def back_keep(v):
    return (v, None)

def back_low(kept, grad):
    return (low(grad),)
low.defvjp(low_keep, low_pass)
low_back.defvjp(back_keep, back_low)

def norm_rows(values, gain_row, shift_row):
    row_mean = lax.optimization_barrier(jnp.mean(values, axis=-1, keepdims=True))
    centred = values - row_mean
    row_var = lax.optimization_barrier(jnp.mean(centred * centred, axis=-1, keepdims=True))
    return centred * lax.rsqrt(row_var + EPSILON) * gain_row + shift_row

def permitted(places):
    count = places.shape[0]
    query_idx = jnp.arange(count, dtype=jnp.int32)[:, None]
    key_idx = jnp.arange(count, dtype=jnp.int32)[None, :]
    return (key_idx <= query_idx) & (key_idx >= query_idx - places[:, None])

def attend_block(packed):
    block_qkv, places = packed
    allowed = permitted(places)[None]
    scores = jnp.einsum('qhd,khd->hqk', block_qkv[:, 0], block_qkv[:, 1], precision=lax.Precision.HIGHEST) * HEAD_DIM ** (-0.5)
    scores = low_back(scores)
    masked = jnp.where(allowed, scores, -jnp.inf)
    row_top = lax.optimization_barrier(jnp.max(masked, axis=-1, keepdims=True))
    expo_vals = jnp.exp(masked - row_top)
    weights_soft = low(expo_vals / lax.optimization_barrier(jnp.sum(expo_vals, axis=-1, keepdims=True)))
    return jnp.einsum('hqk,khd->qhd', weights_soft, block_qkv[:, 2], precision=lax.Precision.HIGHEST)

def one_layer(input_rows, places, w_qkv, w_out, w_up, w_down, gains, shifts, up_bias):
    token_count, feat_width = input_rows.shape
    normed_one = low(norm_rows(input_rows, gains[0], shifts[0]))
    qkv_bias = jnp.concatenate([shifts[1], jnp.zeros_like(shifts[1]), shifts[2]])
    joined = low(low_back(jnp.dot(normed_one, w_qkv, precision=lax.Precision.HIGHEST) + qkv_bias))
    block_count = token_count // SEQ
    heads_qkv = joined.reshape(block_count, SEQ, 3, HEADS, HEAD_DIM)
    attended = lax.map(jax.checkpoint(attend_block), (heads_qkv, places.reshape(block_count, SEQ)))
    mixed_heads = low(low_back(attended.reshape(token_count, feat_width)))
    hidden_one = input_rows + low_back(jnp.dot(mixed_heads, w_out, precision=lax.Precision.HIGHEST) + shifts[3])
    normed_two = low(norm_rows(hidden_one, gains[1], shifts[4]))
    inner_pre = low_back(jnp.dot(normed_two, w_up, precision=lax.Precision.HIGHEST) + up_bias)
    active = low(jax.nn.gelu(inner_pre, approximate=False))
    return hidden_one + low_back(jnp.dot(active, w_down, precision=lax.Precision.HIGHEST) + shifts[5])

def reference(tokens, positions, cotangent, w_qkv, w_out, w_up, w_down, norm_gains, biases, up_bias):

    def section_params(index):
        return (w_qkv[index].astype(jnp.float32), w_out[index].astype(jnp.float32), w_up[index].astype(jnp.float32), w_down[index].astype(jnp.float32), norm_gains[index].astype(jnp.float32), biases[index].astype(jnp.float32), up_bias[index].astype(jnp.float32))

    def run_layer(rows_in, *params):
        return one_layer(rows_in, positions, *params)
    start_rows = tokens.astype(jnp.float32)
    first_out, first_back = jax.vjp(run_layer, start_rows, *section_params(0))
    handed = lax.optimization_barrier(first_out.astype(jnp.bfloat16)).astype(jnp.float32)
    second_out, second_back = jax.vjp(run_layer, handed, *section_params(1))
    second_grads = second_back(cotangent.astype(jnp.float32))
    returned = lax.optimization_barrier(second_grads[0].astype(jnp.bfloat16)).astype(jnp.float32)
    first_grads = first_back(returned)
    section_acts = jnp.stack([first_out.astype(jnp.bfloat16), second_out.astype(jnp.bfloat16)])
    section_grads = jnp.stack([first_grads[0], second_grads[0]])
    return (section_acts, section_grads, jnp.stack([first_grads[1], second_grads[1]]), jnp.stack([first_grads[2], second_grads[2]]), jnp.stack([first_grads[3], second_grads[3]]), jnp.stack([first_grads[4], second_grads[4]]), jnp.stack([first_grads[5], second_grads[5]]), jnp.stack([first_grads[6], second_grads[6]]), jnp.stack([first_grads[7], second_grads[7]]))
```

```python
import jax
import jax.numpy as jnp
from jax import lax
from jax.sharding import PartitionSpec as P

HEAD_DIM = 64
EPSILON = 1e-05
BOTH = ("section", "dp")
F32 = jnp.float32
BF16 = jnp.bfloat16


def norm_rows(values, gain_row, shift_row):
    row_mean = jnp.mean(values, axis=-1, keepdims=True)
    centred = values - row_mean
    row_var = jnp.mean(centred * centred, axis=-1, keepdims=True)
    return centred * lax.rsqrt(row_var + EPSILON) * gain_row + shift_row


def permitted(places):
    count = places.shape[0]
    query_idx = jnp.arange(count, dtype=jnp.int32)[:, None]
    key_idx = jnp.arange(count, dtype=jnp.int32)[None, :]
    return (key_idx <= query_idx) & (key_idx >= query_idx - places[:, None])


def product(left, right):
    return jnp.dot(left, right, preferred_element_type=F32)


def outer_sum(left, right):
    return lax.dot_general(left, right, (((0,), (0,)), ((), ())), preferred_element_type=F32)


def against(left, right):
    return lax.dot_general(left, right, (((1,), (1,)), ((), ())), preferred_element_type=F32)


class Links:
    def __init__(self, data_devices):
        self.count = data_devices
        self.core = lax.axis_index("section")
        self.me = lax.axis_index("dp")
        self.deep = data_devices // 4
        self.staged = data_devices == 16
        quad = self.me % 4
        self.level = self.me // 4
        flip_first = jnp.where(self.core == 0, 2, 1)
        self.quad = quad
        self.quad_first = quad ^ flip_first
        self.quad_second = quad ^ (3 - flip_first)
        self.quad_far = quad ^ 3
        count = data_devices
        index = [(c, d) for c in range(2) for d in range(count)]

        def pairs(move):
            return [(c * count + d, move(c, d)) for c, d in index]

        self.swap = pairs(lambda c, d: (1 - c) * count + d)
        self.first = pairs(lambda c, d: c * count + (d ^ (2 if c == 0 else 1)))
        self.second = pairs(lambda c, d: c * count + (d ^ (1 if c == 0 else 2)))
        self.turns = [
            pairs(lambda c, d, k=k: c * count + (d + 4 * k) % count) for k in range(self.deep)
        ]

    def send(self, x, perm):
        return lax.ppermute(x, BOTH, perm)

    def swap_cores(self, x):
        return self.send(x, self.swap)

    def gather(self, half):
        if not self.staged:
            return lax.all_gather(half, "dp", axis=0)
        deep = self.deep
        turned = [half] + [self.send(half, self.turns[k]) for k in range(1, deep)]
        listed = jnp.stack([turned[(-t) % deep] for t in range(2 * deep)])
        mine = lax.dynamic_slice_in_dim(listed, deep - self.level, deep, 0)
        second = self.send(mine, self.second)
        pair = jnp.stack([mine, second])
        far = self.send(pair, self.first)
        out = jnp.zeros((deep, 4) + half.shape, half.dtype)
        for part, place in (
            (mine, self.quad),
            (second, self.quad_second),
            (far[0], self.quad_first),
            (far[1], self.quad_far),
        ):
            out = lax.dynamic_update_slice_in_dim(out, part[:, None], place, 1)
        return out.reshape((self.count,) + half.shape)

    def reduce(self, total):
        if not self.staged:
            return lax.psum_scatter(total.astype(F32), "dp", scatter_dimension=0)
        deep = self.deep
        shape = total.shape[1:]
        quads = total.reshape((deep, 4) + shape)

        def pick(place):
            return lax.dynamic_slice_in_dim(quads, place, 1, 1)[:, 0]

        arrived = self.send(jnp.stack([pick(self.quad_first), pick(self.quad_far)]), self.first)
        passed = (pick(self.quad_second).astype(F32) + arrived[1].astype(F32)).astype(BF16)
        kept = pick(self.quad).astype(F32) + arrived[0].astype(F32)
        arrived = self.send(passed, self.second)
        kept = (kept + arrived.astype(F32)).astype(BF16)

        def block(step):
            place = (self.level + step) % deep
            return lax.dynamic_slice_in_dim(kept, place, 1, 0)[0]

        result = block(0).astype(F32)
        for k in range(1, deep):
            result = result + self.send(block(k), self.turns[k]).astype(F32)
        return result


def masked_scores(heads_qkv, places):
    scores = jnp.einsum(
        "qhd,khd->hqk", heads_qkv[:, 0], heads_qkv[:, 1], preferred_element_type=F32
    ) * HEAD_DIM ** (-0.5)
    return jnp.where(permitted(places)[None], scores, -jnp.inf)


def attend(joined, places):
    count, wide = joined.shape
    heads_qkv = joined.reshape(count, 3, -1, HEAD_DIM)
    masked = masked_scores(heads_qkv, places)
    row_top = jnp.max(masked, axis=-1, keepdims=True)
    expo_vals = jnp.exp(masked - row_top)
    row_total = jnp.sum(expo_vals, axis=-1, keepdims=True)
    soft_low = (expo_vals / row_total).astype(BF16)
    mixed = jnp.einsum("hqk,khd->qhd", soft_low, heads_qkv[:, 2], preferred_element_type=F32)
    return mixed.reshape(count, wide // 3).astype(BF16), (row_top, row_total)


def attend_back(joined, places, stats, d_mixed):
    count, wide = joined.shape
    row_top, row_total = stats
    heads_qkv = joined.reshape(count, 3, -1, HEAD_DIM)
    d_mixed = d_mixed.reshape(count, -1, HEAD_DIM)
    masked = masked_scores(heads_qkv, places)
    weights_soft = jnp.exp(masked - row_top) / row_total
    soft_low = weights_soft.astype(BF16)
    d_values = jnp.einsum("hqk,qhd->khd", soft_low, d_mixed, preferred_element_type=F32)
    d_soft = jnp.einsum("qhd,khd->hqk", d_mixed, heads_qkv[:, 2], preferred_element_type=F32)
    d_scores = (
        weights_soft * (d_soft - jnp.sum(d_soft * weights_soft, axis=-1, keepdims=True))
    ).astype(BF16)
    scale = HEAD_DIM ** (-0.5)
    d_query = (
        jnp.einsum("hqk,khd->qhd", d_scores, heads_qkv[:, 1], preferred_element_type=F32) * scale
    )
    d_keys = (
        jnp.einsum("hqk,qhd->khd", d_scores, heads_qkv[:, 0], preferred_element_type=F32) * scale
    )
    return jnp.stack([d_query, d_keys, d_values], axis=1).reshape(count, wide).astype(BF16)


def layer_forward(source, places, weights, spread):
    w_qo, w_up, w_down, gains, shifts, up_bias = weights
    feat = source.shape[1]
    rows = source.astype(F32)
    normed_one = norm_rows(rows, gains[0], shifts[0]).astype(BF16)
    normed_one = product(normed_one, spread).astype(BF16)
    bias = jnp.concatenate([shifts[1], jnp.zeros_like(shifts[1]), shifts[2]])
    joined = (product(normed_one, w_qo)[:, : 3 * feat] + bias).astype(BF16)
    mixed, stats = attend(joined, places)
    mixed = product(mixed, spread).astype(BF16)
    w_out = w_qo[:, 3 * feat :]
    hidden_one = rows + (product(mixed, w_out) + shifts[3])
    normed_two = norm_rows(hidden_one, gains[1], shifts[4]).astype(BF16)
    normed_two = product(normed_two, spread).astype(BF16)
    inner = product(normed_two, w_up) + up_bias
    active = jax.nn.gelu(inner, approximate=False).astype(BF16)
    result = (hidden_one + (product(active, w_down) + shifts[5])).astype(BF16)
    return result, (rows, normed_one, joined, stats, mixed, w_out, hidden_one, normed_two, inner, active)


def gather_back(values, spread):
    high = lax.reduce_precision(values, 8, 7)
    low = (values - high).astype(BF16)
    return against(high.astype(BF16), spread) + against(low, spread)


def layer_backward(grad_rows, places, weights, state, spread, ship):
    w_qo, w_up, w_down, gains, shifts, up_bias = weights
    rows, normed_one, joined, stats, mixed, w_out, hidden_one, normed_two, inner, active = state
    count, feat = rows.shape
    data_devices = ship.links.count
    down_in = grad_rows
    ship.down(outer_sum(active, down_in).astype(BF16))
    grad_bdown = jnp.sum(down_in, axis=0, dtype=F32)
    d_active = against(down_in, w_down)
    gelu_back = jax.vjp(lambda v: jax.nn.gelu(v, approximate=False), inner)[1]
    d_inner = gelu_back(d_active)[0].astype(BF16)
    ship.up(normed_two, d_inner)
    grad_bup = jnp.sum(d_inner, axis=0, dtype=F32)
    d_second = gather_back(against(d_inner, w_up), spread)
    second_back = jax.vjp(norm_rows, hidden_one, gains[1], shifts[4])[1]
    d_hidden, grad_gain_two, grad_shift_two = second_back(d_second)
    d_hidden = grad_rows.astype(F32) + d_hidden
    out_in = d_hidden.astype(BF16)
    grad_wout = outer_sum(mixed, out_in)
    grad_bout = jnp.sum(out_in, axis=0, dtype=F32)
    d_mixed = against(out_in, w_out).astype(BF16)
    d_mixed = against(d_mixed, spread).astype(BF16)
    d_joined = attend_back(joined, places, stats, d_mixed)
    grad_wqkv = outer_sum(normed_one, d_joined)
    joined_sums = jnp.sum(d_joined, axis=0, dtype=F32)
    w_qkv_grad = jnp.concatenate([d_joined, jnp.zeros((count, feat), BF16)], axis=1)
    d_first = gather_back(against(w_qkv_grad, w_qo), spread)
    first_back = jax.vjp(norm_rows, rows, gains[0], shifts[0])[1]
    d_input, grad_gain_one, grad_shift_one = first_back(d_first)
    d_input = d_hidden + d_input
    small = [
        grad_gain_one,
        grad_gain_two,
        grad_shift_one,
        joined_sums[:feat],
        joined_sums[2 * feat :],
        grad_bout,
        grad_shift_two,
        grad_bdown,
        grad_bup,
    ]
    small = jnp.concatenate([item.reshape(data_devices, -1) for item in small], axis=1)
    ship.attention(grad_wqkv.astype(BF16), grad_wout.astype(BF16), small)
    return d_input


class Shipper:
    def __init__(self, links, own_rows, pad_rows, cols):
        self.links = links
        self.own = own_rows
        self.pad = pad_rows
        self.cols = cols

    def finish(self, keep, away):
        total = (keep.astype(F32) + self.links.swap_cores(away).astype(F32)).astype(BF16)
        return self.links.reduce(total)

    def down(self, grad):
        core = self.links.core
        grad = grad.reshape(self.links.count, 2, -1, grad.shape[1])
        keep = lax.dynamic_slice_in_dim(grad, core, 1, 1)[:, 0]
        away = lax.dynamic_slice_in_dim(grad, 1 - core, 1, 1)[:, 0]
        self.down_done = self.finish(keep, away)

    def up(self, left, right):
        core = self.links.core
        half = self.cols // 2
        shape = (self.links.count, self.pad, half)
        away = outer_sum(left, lax.dynamic_slice_in_dim(right, (1 - core) * half, half, 1))
        keep = outer_sum(left, lax.dynamic_slice_in_dim(right, core * half, half, 1))
        self.up_done = self.finish(
            keep.astype(BF16).reshape(shape), away.astype(BF16).reshape(shape)
        )

    def attention(self, grad_qkv, grad_out, small):
        core = self.links.core
        half = self.cols // 2
        grad = jnp.concatenate([grad_qkv, grad_out], axis=1)
        grad = grad.reshape(self.links.count, self.pad, self.cols)
        small = jnp.pad(small.astype(BF16), ((0, 0), (0, self.cols - small.shape[1])))
        row = lax.broadcasted_iota(jnp.int32, grad.shape, 1)
        grad = jnp.where(row == self.own, small[:, None, :], grad)
        keep = lax.dynamic_slice_in_dim(grad, core * half, half, 2)
        away = lax.dynamic_slice_in_dim(grad, (1 - core) * half, half, 2)
        self.attention_done = self.finish(keep, away)


def per_device(
    tokens, positions, cotangent, w_qkv, w_out, w_up, w_down, norm_gains, biases, up_bias
):
    data_devices = lax.axis_size("dp")
    links = Links(data_devices)
    core = links.core
    own = w_qkv.shape[1]
    pad = (own // 8 + 1) * 8
    feat = own * data_devices
    cols = w_up.shape[2]
    half = cols // 2
    count = tokens.shape[0] // 2

    feature = lax.broadcasted_iota(jnp.int32, (feat, pad * data_devices), 0)
    column = lax.broadcasted_iota(jnp.int32, (feat, pad * data_devices), 1)
    spread = (column == feature // own * pad + feature % own).astype(BF16)

    small = jnp.concatenate([norm_gains[0].reshape(-1), biases[0].reshape(-1), up_bias[0]])
    small_size = small.shape[0]
    small = jnp.pad(small, (0, cols - small_size))[None]
    shard_qo = jnp.concatenate([w_qkv[0], w_out[0]], axis=1)
    shard_qo = jnp.concatenate([shard_qo, small, jnp.zeros((pad - own - 1, cols), BF16)], axis=0)
    shard_up = jnp.pad(w_up[0], ((0, pad - own), (0, 0)))
    shard_down = w_down[0]
    down_half = shard_down.shape[0] // 2

    def own_halves(shard, size, axis):
        keep = lax.dynamic_slice_in_dim(shard, core * size, size, axis)
        away = lax.dynamic_slice_in_dim(shard, (1 - core) * size, size, axis)
        other = links.swap_cores(away)
        return (jnp.where(core == 0, keep, other), jnp.where(core == 0, other, keep))

    halves_qo = own_halves(shard_qo, half, 1)
    halves_up = own_halves(shard_up, half, 1)
    halves_down = own_halves(shard_down, down_half, 0)

    def whole(part, axis):
        other = links.swap_cores(part)
        shape = part.shape[:axis] + (2 * part.shape[axis],) + part.shape[axis + 1 :]
        out = jnp.zeros(shape, part.dtype)
        size = part.shape[axis]
        out = lax.dynamic_update_slice_in_dim(out, part, core * size, axis)
        return lax.dynamic_update_slice_in_dim(out, other, (1 - core) * size, axis)

    layers = []
    for layer in range(2):
        qo = whole(links.gather(halves_qo[layer]), 2)
        up = whole(links.gather(halves_up[layer]), 2)
        down = links.gather(halves_down[layer])
        down = whole(down[:, None], 1).reshape(-1, feat)
        smalls = qo[:, own, :small_size].astype(F32)
        gains = smalls[:, : 2 * own].reshape(data_devices, 2, own)
        gains = gains.transpose(1, 0, 2).reshape(2, feat)
        shifts = smalls[:, 2 * own : 8 * own].reshape(data_devices, 6, own)
        shifts = shifts.transpose(1, 0, 2).reshape(6, feat)
        bias = smalls[:, 8 * own :].reshape(-1)
        layers.append(
            (qo.reshape(-1, cols), up.reshape(-1, cols), down, gains, shifts, bias)
        )

    source = lax.dynamic_slice_in_dim(tokens, core * count, count)
    places = lax.dynamic_slice_in_dim(positions, core * count, count)
    cotan = lax.dynamic_slice_in_dim(cotangent, core * count, count)
    first_out, first_state = layer_forward(source, places, layers[0], spread)
    second_out, second_state = layer_forward(first_out, places, layers[1], spread)
    ships = [Shipper(links, own, pad, cols) for _ in range(2)]
    second_grad = layer_backward(cotan, places, layers[1], second_state, spread, ships[1])
    first_grad = layer_backward(
        second_grad.astype(BF16), places, layers[0], first_state, spread, ships[0]
    )

    def by_layer(first, second):
        mine = jnp.where(core == 0, first, second)
        other = links.swap_cores(jnp.where(core == 0, second, first))
        return jnp.where(core == 0, mine, other), jnp.where(core == 0, other, mine)

    acts = jnp.concatenate(by_layer(first_out, second_out), axis=0)[None]
    grads = jnp.concatenate(by_layer(first_grad, second_grad), axis=0)[None]

    qo = jnp.concatenate(by_layer(ships[0].attention_done, ships[1].attention_done), axis=1)
    up = jnp.concatenate(by_layer(ships[0].up_done, ships[1].up_done), axis=1)
    down = jnp.concatenate(by_layer(ships[0].down_done, ships[1].down_done), axis=0)
    smalls = qo[own, :small_size]
    return (
        acts,
        grads,
        qo[None, :own, : 3 * feat],
        qo[None, :own, 3 * feat :],
        up[None, :own],
        down[None],
        smalls[: 2 * own].reshape(1, 2, own),
        smalls[2 * own : 8 * own].reshape(1, 6, own),
        smalls[8 * own :][None],
    )


def solution(mesh):
    rows = P("dp", None)
    weight = P("section", "dp", None)
    vector = P("section", None, "dp")
    in_specs = (rows, P("dp"), rows, weight, weight, weight, weight, vector, vector, P("section", "dp"))
    out_specs = (weight, weight, weight, weight, weight, weight, vector, vector, P("section", "dp"))
    return jax.shard_map(
        per_device, mesh=mesh, in_specs=in_specs, out_specs=out_specs, check_vma=False
    )
```

```python
import jax
import jax.numpy as jnp
from jax import lax
from jax.sharding import PartitionSpec as P

HEAD_DIM = 64
EPSILON = 1e-05
BOTH = ("section", "dp")
F32 = jnp.float32
BF16 = jnp.bfloat16


def norm_rows(values, gain_row, shift_row):
    row_mean = jnp.mean(values, axis=-1, keepdims=True)
    centred = values - row_mean
    row_var = jnp.mean(centred * centred, axis=-1, keepdims=True)
    return centred * lax.rsqrt(row_var + EPSILON) * gain_row + shift_row


def permitted(places):
    count = places.shape[0]
    query_idx = jnp.arange(count, dtype=jnp.int32)[:, None]
    key_idx = jnp.arange(count, dtype=jnp.int32)[None, :]
    return (key_idx <= query_idx) & (key_idx >= query_idx - places[:, None])


def product(left, right):
    return jnp.dot(left, right, preferred_element_type=F32)


def outer_sum(left, right):
    return lax.dot_general(left, right, (((0,), (0,)), ((), ())), preferred_element_type=F32)


def against(left, right):
    return lax.dot_general(left, right, (((1,), (1,)), ((), ())), preferred_element_type=F32)


class Links:
    def __init__(self, data_devices):
        self.count = data_devices
        self.core = lax.axis_index("section")
        self.me = lax.axis_index("dp")
        self.deep = data_devices // 4
        self.staged = data_devices == 16
        self.quad = self.me % 4
        self.level = self.me // 4
        count = data_devices
        index = [(c, d) for c in range(2) for d in range(count)]

        def pairs(move):
            return [(c * count + d, move(c, d)) for c, d in index]

        self.swap = pairs(lambda c, d: (1 - c) * count + d)
        self.first = pairs(lambda c, d: c * count + (d ^ (2 if c == 0 else 1)))
        self.second = pairs(lambda c, d: c * count + (d ^ (1 if c == 0 else 2)))
        self.turns = [
            pairs(lambda c, d, k=k: c * count + (d + 4 * k) % count) for k in range(self.deep)
        ]

    def send(self, x, perm):
        return lax.ppermute(x, BOTH, perm)

    def swap_cores(self, x):
        return self.send(x, self.swap)

    def flips(self, core):
        first = jnp.where(core == 0, 2, 1)
        return [0, 3 - first, first, 3]

    def order(self, core):
        if not self.staged:
            return jnp.arange(self.count)
        quads = self.quad ^ jnp.stack([jnp.int32(v) for v in self.flips(core)])
        levels = (self.level - jnp.arange(self.deep)) % self.deep
        return (levels[None, :] * 4 + quads[:, None]).reshape(-1)


class Gather:
    def __init__(self, links, half, sorted_blocks):
        self.links = links
        self.sorted = sorted_blocks
        self.shape = half.shape
        self.live = [half]

    def stage_turn(self):
        links, (half,) = self.links, self.live
        if not links.staged:
            return
        deep = links.deep
        turned = [half] + [links.send(half, links.turns[k]) for k in range(1, deep)]
        if self.sorted:
            listed = jnp.stack([turned[(-t) % deep] for t in range(2 * deep)])
            self.live = [lax.dynamic_slice_in_dim(listed, deep - links.level, deep, 0)]
        else:
            self.live = [jnp.stack(turned)]

    def stage_second(self):
        if self.links.staged:
            (mine,) = self.live
            self.live = [jnp.stack([mine, self.links.send(mine, self.links.second)])]

    def stage_first(self):
        links = self.links
        if not links.staged:
            self.live = [lax.all_gather(self.live[0], "dp", axis=0)]
            return
        (pair,) = self.live
        parts = [pair, links.send(pair, links.first)]
        if not self.sorted:
            self.live = [jnp.concatenate(parts, axis=0)]
            return
        out = jnp.zeros((links.deep, 4) + self.shape, pair.dtype)
        for place, flip in enumerate(links.flips(links.core)):
            part = parts[place // 2][place % 2]
            out = lax.dynamic_update_slice_in_dim(out, part[:, None], links.quad ^ flip, 1)
        self.live = [out]

    def stage_swap(self):
        (mine,) = self.live
        mine = mine.reshape(-1, self.shape[1])
        self.mine, self.other = mine, self.links.swap_cores(mine)
        self.live = []


class Reduce:
    def __init__(self, links, keep, away, sorted_blocks):
        self.links = links
        self.sorted = sorted_blocks
        shape = (links.count, -1, keep.shape[1])
        self.live = [keep.reshape(shape), away.reshape(shape)]

    def stage_swap(self):
        keep, away = self.live
        total = (keep.astype(F32) + self.links.swap_cores(away).astype(F32)).astype(BF16)
        self.live = [total]

    def stage_first(self):
        links, (total,) = self.links, self.live
        if not links.staged:
            self.live = [lax.psum_scatter(total.astype(F32), "dp", scatter_dimension=0)]
            return
        shape = total.shape[1:]
        if self.sorted:
            quads = total.reshape((links.deep, 4) + shape)
            kept, passed, one, two = [
                lax.dynamic_slice_in_dim(quads, links.quad ^ flip, 1, 1)[:, 0]
                for flip in links.flips(links.core)
            ]
            away = jnp.stack([one, two])
        else:
            quads = total.reshape((4, links.deep) + shape)
            kept, passed, away = quads[0], quads[1], quads[2:]
        arrived = links.send(away, links.first)
        passed = (passed.astype(F32) + arrived[1].astype(F32)).astype(BF16)
        kept = (kept.astype(F32) + arrived[0].astype(F32)).astype(BF16)
        self.live = [kept, passed]

    def stage_second(self):
        if self.links.staged:
            kept, passed = self.live
            arrived = self.links.send(passed, self.links.second)
            self.live = [(kept.astype(F32) + arrived.astype(F32)).astype(BF16)]

    def stage_turn(self):
        links, (kept,) = self.links, self.live
        if links.staged:
            deep = links.deep

            def block(step):
                if not self.sorted:
                    return kept[step]
                place = (links.level + deep - step) % deep
                return lax.dynamic_slice_in_dim(kept, place, 1, 0)[0]

            result = block(0).astype(F32)
            for k in range(1, deep):
                result = result + links.send(block(k), links.turns[deep - k]).astype(F32)
            self.live = [result]


def fence(jobs, others):
    held = lax.optimization_barrier(([job.live for job in jobs], others))
    for job, live in zip(jobs, held[0]):
        job.live = live
    return held[1]


def masked_scores(heads_qkv, places):
    scores = jnp.einsum(
        "qhd,khd->hqk", heads_qkv[:, 0], heads_qkv[:, 1], preferred_element_type=F32
    ) * HEAD_DIM ** (-0.5)
    return jnp.where(permitted(places)[None], scores, -jnp.inf)


def attend(joined, places):
    count, wide = joined.shape
    heads_qkv = joined.reshape(count, 3, -1, HEAD_DIM)
    masked = masked_scores(heads_qkv, places)
    row_top = jnp.max(masked, axis=-1, keepdims=True)
    expo_vals = jnp.exp(masked - row_top)
    row_total = jnp.sum(expo_vals, axis=-1, keepdims=True)
    soft_low = (expo_vals / row_total).astype(BF16)
    mixed = jnp.einsum("hqk,khd->qhd", soft_low, heads_qkv[:, 2], preferred_element_type=F32)
    return mixed.reshape(count, wide // 3).astype(BF16), (row_top, row_total)


def attend_back(joined, places, stats, d_mixed):
    count, wide = joined.shape
    row_top, row_total = stats
    heads_qkv = joined.reshape(count, 3, -1, HEAD_DIM)
    d_mixed = d_mixed.reshape(count, -1, HEAD_DIM)
    masked = masked_scores(heads_qkv, places)
    weights_soft = jnp.exp(masked - row_top) / row_total
    soft_low = weights_soft.astype(BF16)
    d_values = jnp.einsum("hqk,qhd->khd", soft_low, d_mixed, preferred_element_type=F32)
    d_soft = jnp.einsum("qhd,khd->hqk", d_mixed, heads_qkv[:, 2], preferred_element_type=F32)
    d_scores = (
        weights_soft * (d_soft - jnp.sum(d_soft * weights_soft, axis=-1, keepdims=True))
    ).astype(BF16)
    scale = HEAD_DIM ** (-0.5)
    d_query = (
        jnp.einsum("hqk,khd->qhd", d_scores, heads_qkv[:, 1], preferred_element_type=F32) * scale
    )
    d_keys = (
        jnp.einsum("hqk,qhd->khd", d_scores, heads_qkv[:, 0], preferred_element_type=F32) * scale
    )
    return jnp.stack([d_query, d_keys, d_values], axis=1).reshape(count, wide).astype(BF16)


def gather_back(values, spread):
    high = lax.reduce_precision(values, 8, 7)
    low = (values - high).astype(BF16)
    return against(high.astype(BF16), spread) + against(low, spread)


def per_device(
    tokens, positions, cotangent, w_qkv, w_out, w_up, w_down, norm_gains, biases, up_bias
):
    data_devices = lax.axis_size("dp")
    links = Links(data_devices)
    core = links.core
    own = w_qkv.shape[1]
    pad = (own // 8 + 1) * 8
    feat = own * data_devices
    wide = pad * data_devices
    cols = w_up.shape[2]
    half = cols // 2
    count = tokens.shape[0] // 2
    down_half = w_down.shape[1] // 2

    def pick(if_first, if_second):
        return jnp.where(core == 0, if_first, if_second)

    orders = [links.order(core), links.order(1 - core)]

    def spread_of(order):
        column = jnp.arange(wide)
        place = column % pad
        target = jnp.where(place < own, jnp.repeat(order, pad) * own + place, -1)
        feature = lax.broadcasted_iota(jnp.int32, (feat, wide), 0)
        return (feature == target[None, :]).astype(BF16)

    spreads = [spread_of(order) for order in orders]
    spread_out = pick(spreads[1], spreads[0])
    order_small = pick(orders[0], orders[1])
    device = jnp.arange(data_devices)[:, None]
    to_device = (device == order_small[None, :]).astype(BF16)

    def halves_first(x):
        lead = x.shape[:-1]
        return x.reshape(lead + (data_devices, 2, down_half)).swapaxes(-3, -2).reshape(lead + (cols,))

    def halves_last(x):
        lead = x.shape[:-1]
        return x.reshape(lead + (2, data_devices, down_half)).swapaxes(-3, -2).reshape(lead + (cols,))

    small = jnp.concatenate([norm_gains[0].reshape(-1), biases[0].reshape(-1), up_bias[0]])
    small_size = small.shape[0]
    small = jnp.pad(small, (0, cols - small_size))[None]
    shard_qo = jnp.concatenate([w_qkv[0, :, : 2 * feat], w_out[0], w_qkv[0, :, 2 * feat :]], axis=1)
    shard_qo = jnp.concatenate([shard_qo, small, jnp.zeros((pad - own - 1, cols), BF16)], axis=0)
    shard_up = halves_first(jnp.pad(w_up[0], ((0, pad - own), (0, 0))))
    shard_down = w_down[0]

    def own_halves(shard, size, axis):
        keep = lax.dynamic_slice_in_dim(shard, core * size, size, axis)
        away = lax.dynamic_slice_in_dim(shard, (1 - core) * size, size, axis)
        other = links.swap_cores(away)
        return (pick(keep, other), pick(other, keep))

    halves_qo = own_halves(shard_qo, half, 1)
    halves_up = own_halves(shard_up, half, 1)
    halves_down = own_halves(shard_down, down_half, 0)
    gathers = []
    for layer in range(2):
        gathers.append(Gather(links, halves_qo[layer], False))
        gathers.append(Gather(links, halves_up[layer], False))
        gathers.append(Gather(links, halves_down[layer], True))

    source = lax.dynamic_slice_in_dim(tokens, core * count, count)
    places = lax.dynamic_slice_in_dim(positions, core * count, count)
    cotan = lax.dynamic_slice_in_dim(cotangent, core * count, count)
    states = [{}, {}]

    def forward_attention(layer, rows_in):
        s = states[layer]
        qo = gathers[3 * layer]
        weights = [qo.mine, qo.other]
        smalls = pick(qo.mine, qo.other).reshape(data_devices, pad, half)[:, own, :small_size]
        smalls = product(to_device, smalls)
        gains = smalls[:, : 2 * own].reshape(data_devices, 2, own)
        gains = gains.transpose(1, 0, 2).reshape(2, feat)
        shifts = smalls[:, 2 * own : 8 * own].reshape(data_devices, 6, own)
        shifts = shifts.transpose(1, 0, 2).reshape(6, feat)
        bias = halves_first(smalls[:, 8 * own :].reshape(-1))
        rows = rows_in.astype(F32)
        normed = norm_rows(rows, gains[0], shifts[0]).astype(BF16)
        normed = [product(normed, spread).astype(BF16) for spread in spreads]
        both = [product(normed[i], weights[i]) for i in range(2)]
        queries = pick(both[0], both[1])
        values = pick(both[1], both[0])[:, feat:]
        joined = jnp.concatenate(
            [queries[:, :feat] + shifts[1], queries[:, feat:], values + shifts[2]], axis=1
        ).astype(BF16)
        mixed, stats = attend(joined, places)
        mixed = product(mixed, spread_out).astype(BF16)
        w_out_all = pick(weights[1], weights[0])[:, :feat]
        hidden = rows + (product(mixed, w_out_all) + shifts[3])
        s.update(
            weights=weights, gains=gains, shifts=shifts, bias=bias, rows=rows, normed_one=normed,
            joined=joined, stats=stats, mixed=mixed, w_out=w_out_all, hidden=hidden,
        )
        return hidden

    def forward_up(layer):
        s = states[layer]
        up = gathers[3 * layer + 1]
        s["up"] = [up.mine, up.other]
        normed = norm_rows(s["hidden"], s["gains"][1], s["shifts"][4]).astype(BF16)
        s["normed_two"] = [product(normed, spread).astype(BF16) for spread in spreads]
        bias = s["bias"]
        bias = [pick(bias[:half], bias[half:]), pick(bias[half:], bias[:half])]
        s["inner"] = [product(s["normed_two"][i], s["up"][i]) + bias[i] for i in range(2)]
        s["active"] = [jax.nn.gelu(v, approximate=False).astype(BF16) for v in s["inner"]]
        return s["active"]

    def forward_down(layer):
        s = states[layer]
        down = gathers[3 * layer + 2]
        s["down"] = [down.mine, down.other]
        total = sum(product(s["active"][i], s["down"][i]) for i in range(2))
        return (s["hidden"] + (total + s["shifts"][5])).astype(BF16)

    def advance(jobs, slot, stages):
        for back, stage in enumerate(stages):
            if 0 <= slot - back < len(jobs):
                getattr(jobs[slot - back], stage)()

    going = ("stage_turn", "stage_second", "stage_first", "stage_swap")
    for slot in range(4):
        advance(gathers, slot, going)
        fence(gathers, ())
    advance(gathers, 4, going)
    fence(gathers, forward_attention(0, source))
    advance(gathers, 5, going)
    fence(gathers, forward_up(0))
    advance(gathers, 6, going)
    first_out = forward_down(0)
    fence(gathers, first_out)
    advance(gathers, 7, going)
    fence(gathers, forward_attention(1, first_out))
    advance(gathers, 8, going)
    forward_up(1)
    second_out = forward_down(1)

    def backward_down(layer, grad_rows):
        s = states[layer]
        grads = [outer_sum(s["active"][i], grad_rows).astype(BF16) for i in range(2)]
        s["grad_bdown"] = jnp.sum(grad_rows, axis=0, dtype=F32)
        s["d_inner"] = []
        for i in range(2):
            d_active = against(grad_rows, s["down"][i])
            back = jax.vjp(lambda v: jax.nn.gelu(v, approximate=False), s["inner"][i])[1]
            s["d_inner"].append(back(d_active)[0].astype(BF16))
        return Reduce(links, grads[0], grads[1], True), s["d_inner"]

    def backward_up(layer, grad_rows):
        s = states[layer]
        d_inner = s["d_inner"]
        grads = [outer_sum(s["normed_two"][i], d_inner[i]).astype(BF16) for i in range(2)]
        bups = [jnp.sum(d, axis=0, dtype=F32) for d in d_inner]
        s["grad_bup"] = halves_last(
            jnp.concatenate([pick(bups[0], bups[1]), pick(bups[1], bups[0])])
        )
        d_second = sum(gather_back(against(d_inner[i], s["up"][i]), spreads[i]) for i in range(2))
        back = jax.vjp(norm_rows, s["hidden"], s["gains"][1], s["shifts"][4])[1]
        d_hidden, s["grad_gain_two"], s["grad_shift_two"] = back(d_second)
        d_hidden = grad_rows.astype(F32) + d_hidden
        return Reduce(links, grads[0], grads[1], False), d_hidden

    def backward_attention(layer, d_hidden):
        s = states[layer]
        out_in = d_hidden.astype(BF16)
        grad_bout = jnp.sum(out_in, axis=0, dtype=F32)
        d_mixed = against(out_in, s["w_out"]).astype(BF16)
        d_mixed = against(d_mixed, spread_out).astype(BF16)
        d_joined = attend_back(s["joined"], places, s["stats"], d_mixed)
        sums = jnp.sum(d_joined, axis=0, dtype=F32)
        d_query, d_key, d_value = (d_joined[:, i * feat : (i + 1) * feat] for i in range(3))
        lone = jnp.zeros_like(d_value)
        kept = jnp.concatenate([d_query, d_key], axis=1)
        rest = jnp.concatenate([lone, d_value], axis=1)
        weights = s["weights"]
        d_first = gather_back(against(pick(kept, rest), weights[0]), spreads[0])
        d_first = d_first + gather_back(against(pick(rest, kept), weights[1]), spreads[1])
        back = jax.vjp(norm_rows, s["rows"], s["gains"][0], s["shifts"][0])[1]
        d_input, grad_gain_one, grad_shift_one = back(d_first)
        d_input = d_hidden + d_input
        small = [
            grad_gain_one, s["grad_gain_two"], grad_shift_one, sums[:feat], sums[2 * feat :],
            grad_bout, s["grad_shift_two"], s["grad_bdown"], s["grad_bup"],
        ]
        small = jnp.concatenate([v.reshape(data_devices, -1) for v in small], axis=1)
        small = outer_sum(to_device, small.astype(BF16)).astype(BF16)
        small = jnp.pad(small, ((0, 0), (0, half - small_size)))
        grads = []
        for i in range(2):
            has_query = core == i
            normed = s["normed_one"][i]
            left = jnp.concatenate([jnp.where(has_query, normed, s["mixed"]), normed], axis=0)
            one = jnp.where(has_query, d_query, out_in)
            two = jnp.where(has_query, d_key, d_value)
            right = jnp.concatenate(
                [jnp.concatenate([one, lone], axis=1), jnp.concatenate([lone, two], axis=1)], axis=0
            )
            grad = outer_sum(left, right).astype(BF16).reshape(data_devices, pad, half)
            row = lax.broadcasted_iota(jnp.int32, grad.shape, 1)
            grad = jnp.where((row == own) & has_query, small[:, None, :], grad)
            grads.append(grad.reshape(wide, half))
        return Reduce(links, grads[0], grads[1], False), d_input

    reduces = []
    returning = ("", "stage_swap", "stage_first", "stage_second", "stage_turn")

    def turn_back(slot, result):
        job, out = result
        reduces.append(job)
        for back in range(1, 5):
            if 0 <= slot - back < len(reduces):
                getattr(reduces[slot - back], returning[back])()
        return fence(reduces, out)

    slot = 0
    grad_in = cotan
    d_inputs = []
    for layer in (1, 0):
        states[layer]["d_inner"] = turn_back(slot, backward_down(layer, grad_in))
        d_hidden = turn_back(slot + 1, backward_up(layer, grad_in))
        d_input = turn_back(slot + 2, backward_attention(layer, d_hidden))
        d_inputs.append(d_input)
        grad_in = d_input.astype(BF16)
        slot += 3
    second_grad, first_grad = d_inputs
    for slot in range(6, 10):
        for back in range(1, 5):
            if 0 <= slot - back < len(reduces):
                getattr(reduces[slot - back], returning[back])()
        fence(reduces, ())
    down_second, up_second, qo_second, down_first, up_first, qo_first = [r.live[0] for r in reduces]

    def by_layer(first, second):
        mine = pick(first, second)
        other = links.swap_cores(pick(second, first))
        return pick(mine, other), pick(other, mine)

    acts = jnp.concatenate(by_layer(first_out, second_out), axis=0)[None]
    grads = jnp.concatenate(by_layer(first_grad, second_grad), axis=0)[None]
    query_key, out_value = [v.reshape(pad, half) for v in by_layer(qo_first, qo_second)]
    up = jnp.concatenate([v.reshape(pad, half) for v in by_layer(up_first, up_second)], axis=1)
    down = by_layer(down_first, down_second)
    down = jnp.concatenate([v.reshape(down_half, feat) for v in down], axis=0)
    smalls = query_key[own, :small_size]
    return (
        acts,
        grads,
        jnp.concatenate([query_key[:own], out_value[:own, feat:]], axis=1)[None],
        out_value[None, :own, :feat],
        halves_last(up[:own])[None],
        down[None],
        smalls[: 2 * own].reshape(1, 2, own),
        smalls[2 * own : 8 * own].reshape(1, 6, own),
        smalls[8 * own :][None],
    )


def solution(mesh):
    rows = P("dp", None)
    weight = P("section", "dp", None)
    vector = P("section", None, "dp")
    in_specs = (rows, P("dp"), rows, weight, weight, weight, weight, vector, vector, P("section", "dp"))
    out_specs = (weight, weight, weight, weight, weight, weight, vector, vector, P("section", "dp"))
    return jax.shard_map(
        per_device, mesh=mesh, in_specs=in_specs, out_specs=out_specs, check_vma=False
    )
```

```python
import jax
import jax.numpy as jnp
from jax import lax
from jax.sharding import PartitionSpec as P

HEAD_DIM = 64
EPSILON = 1e-05
BOTH = ("section", "dp")
F32 = jnp.float32
BF16 = jnp.bfloat16


def norm_rows(values, gain_row, shift_row):
    row_mean = jnp.mean(values, axis=-1, keepdims=True)
    centred = values - row_mean
    row_var = jnp.mean(centred * centred, axis=-1, keepdims=True)
    return centred * lax.rsqrt(row_var + EPSILON) * gain_row + shift_row


def permitted(places):
    count = places.shape[0]
    query_idx = jnp.arange(count, dtype=jnp.int32)[:, None]
    key_idx = jnp.arange(count, dtype=jnp.int32)[None, :]
    return (key_idx <= query_idx) & (key_idx >= query_idx - places[:, None])


def product(left, right):
    return jnp.dot(left, right, preferred_element_type=F32)


def outer_sum(left, right):
    return lax.dot_general(left, right, (((0,), (0,)), ((), ())), preferred_element_type=F32)


def against(left, right):
    return lax.dot_general(left, right, (((1,), (1,)), ((), ())), preferred_element_type=F32)


class Links:
    def __init__(self, data_devices):
        self.count = data_devices
        self.core = lax.axis_index("section")
        self.me = lax.axis_index("dp")
        self.deep = data_devices // 4
        self.staged = data_devices == 16
        self.quad = self.me % 4
        self.level = self.me // 4
        count = data_devices
        index = [(c, d) for c in range(2) for d in range(count)]

        def pairs(move):
            return [(c * count + d, move(c, d)) for c, d in index]

        self.swap = pairs(lambda c, d: (1 - c) * count + d)
        self.first = pairs(lambda c, d: c * count + (d ^ (2 if c == 0 else 1)))
        self.second = pairs(lambda c, d: c * count + (d ^ (1 if c == 0 else 2)))
        self.turns = [
            pairs(lambda c, d, k=k: c * count + (d + 4 * k) % count) for k in range(self.deep)
        ]

    def send(self, x, perm):
        return lax.ppermute(x, BOTH, perm)

    def swap_cores(self, x):
        return self.send(x, self.swap)

    def flips(self, core):
        first = jnp.where(core == 0, 2, 1)
        return [0, 3 - first, first, 3]

    def order(self, core):
        if not self.staged:
            return jnp.arange(self.count)
        quads = self.quad ^ jnp.stack([jnp.int32(v) for v in self.flips(core)])
        levels = (self.level - jnp.arange(self.deep)) % self.deep
        return (levels[None, :] * 4 + quads[:, None]).reshape(-1)


class Gather:
    def __init__(self, links, half, sorted_blocks):
        self.links = links
        self.sorted = sorted_blocks
        self.shape = half.shape
        self.live = [half]

    def stage_turn(self):
        links, (half,) = self.links, self.live
        if not links.staged:
            return
        deep = links.deep
        turned = [half] + [links.send(half, links.turns[k]) for k in range(1, deep)]
        if self.sorted:
            listed = jnp.stack([turned[(-t) % deep] for t in range(2 * deep)])
            self.live = [lax.dynamic_slice_in_dim(listed, deep - links.level, deep, 0)]
        else:
            self.live = [jnp.stack(turned)]

    def stage_second(self):
        if self.links.staged:
            (mine,) = self.live
            self.live = [jnp.stack([mine, self.links.send(mine, self.links.second)])]

    def stage_first(self):
        links = self.links
        if not links.staged:
            self.live = [lax.all_gather(self.live[0], "dp", axis=0)]
            return
        (pair,) = self.live
        parts = [pair, links.send(pair, links.first)]
        if not self.sorted:
            self.live = [jnp.concatenate(parts, axis=0)]
            return
        out = jnp.zeros((links.deep, 4) + self.shape, pair.dtype)
        for place, flip in enumerate(links.flips(links.core)):
            part = parts[place // 2][place % 2]
            out = lax.dynamic_update_slice_in_dim(out, part[:, None], links.quad ^ flip, 1)
        self.live = [out]

    def stage_swap(self):
        (mine,) = self.live
        mine = mine.reshape(-1, self.shape[1])
        self.live = [mine, self.links.swap_cores(mine)]


class Reduce:
    def __init__(self, links, keep, away, sorted_blocks):
        self.links = links
        self.sorted = sorted_blocks
        shape = (links.count, -1, keep.shape[1])
        self.live = [keep.reshape(shape), away.reshape(shape)]

    def stage_swap(self):
        keep, away = self.live
        total = (keep.astype(F32) + self.links.swap_cores(away).astype(F32)).astype(BF16)
        self.live = [total]

    def stage_first(self):
        links, (total,) = self.links, self.live
        if not links.staged:
            self.live = [lax.psum_scatter(total.astype(F32), "dp", scatter_dimension=0)]
            return
        shape = total.shape[1:]
        if self.sorted:
            quads = total.reshape((links.deep, 4) + shape)
            kept, passed, one, two = [
                lax.dynamic_slice_in_dim(quads, links.quad ^ flip, 1, 1)[:, 0]
                for flip in links.flips(links.core)
            ]
            away = jnp.stack([one, two])
        else:
            quads = total.reshape((4, links.deep) + shape)
            kept, passed, away = quads[0], quads[1], quads[2:]
        arrived = links.send(away, links.first)
        passed = (passed.astype(F32) + arrived[1].astype(F32)).astype(BF16)
        kept = (kept.astype(F32) + arrived[0].astype(F32)).astype(BF16)
        self.live = [kept, passed]

    def stage_second(self):
        if self.links.staged:
            kept, passed = self.live
            arrived = self.links.send(passed, self.links.second)
            self.live = [(kept.astype(F32) + arrived.astype(F32)).astype(BF16)]

    def stage_turn(self):
        links, (kept,) = self.links, self.live
        if links.staged:
            deep = links.deep

            def block(step):
                if not self.sorted:
                    return kept[step]
                place = (links.level + deep - step) % deep
                return lax.dynamic_slice_in_dim(kept, place, 1, 0)[0]

            result = block(0).astype(F32)
            for k in range(1, deep):
                result = result + links.send(block(k), links.turns[deep - k]).astype(F32)
            self.live = [result]


def fence(jobs, others):
    held = lax.optimization_barrier(([job.live for job in jobs], others))
    for job, live in zip(jobs, held[0]):
        job.live = live
    return held[1]


def masked_scores(heads_qkv, places):
    scores = jnp.einsum(
        "qhd,khd->hqk", heads_qkv[:, 0], heads_qkv[:, 1], preferred_element_type=F32
    ) * HEAD_DIM ** (-0.5)
    return jnp.where(permitted(places)[None], scores, -jnp.inf)


def attend(joined, places):
    count, wide = joined.shape
    heads_qkv = joined.reshape(count, 3, -1, HEAD_DIM)
    masked = masked_scores(heads_qkv, places)
    row_top = jnp.max(masked, axis=-1, keepdims=True)
    expo_vals = jnp.exp(masked - row_top)
    row_total = jnp.sum(expo_vals, axis=-1, keepdims=True)
    soft_low = (expo_vals / row_total).astype(BF16)
    mixed = jnp.einsum("hqk,khd->qhd", soft_low, heads_qkv[:, 2], preferred_element_type=F32)
    return mixed.reshape(count, wide // 3).astype(BF16), (row_top, row_total)


def attend_back(joined, places, stats, d_mixed):
    count, wide = joined.shape
    row_top, row_total = stats
    heads_qkv = joined.reshape(count, 3, -1, HEAD_DIM)
    d_mixed = d_mixed.reshape(count, -1, HEAD_DIM)
    masked = masked_scores(heads_qkv, places)
    weights_soft = jnp.exp(masked - row_top) / row_total
    soft_low = weights_soft.astype(BF16)
    d_values = jnp.einsum("hqk,qhd->khd", soft_low, d_mixed, preferred_element_type=F32)
    d_soft = jnp.einsum("qhd,khd->hqk", d_mixed, heads_qkv[:, 2], preferred_element_type=F32)
    d_scores = (
        weights_soft * (d_soft - jnp.sum(d_soft * weights_soft, axis=-1, keepdims=True))
    ).astype(BF16)
    scale = HEAD_DIM ** (-0.5)
    d_query = (
        jnp.einsum("hqk,khd->qhd", d_scores, heads_qkv[:, 1], preferred_element_type=F32) * scale
    )
    d_keys = (
        jnp.einsum("hqk,qhd->khd", d_scores, heads_qkv[:, 0], preferred_element_type=F32) * scale
    )
    return jnp.stack([d_query, d_keys, d_values], axis=1).reshape(count, wide).astype(BF16)


def gather_back(values, spread):
    high = lax.reduce_precision(values, 8, 7)
    low = (values - high).astype(BF16)
    return against(high.astype(BF16), spread) + against(low, spread)


def per_device(
    tokens, positions, cotangent, w_qkv, w_out, w_up, w_down, norm_gains, biases, up_bias
):
    data_devices = lax.axis_size("dp")
    links = Links(data_devices)
    core = links.core
    own = w_qkv.shape[1]
    pad = (own // 8 + 1) * 8
    feat = own * data_devices
    wide = pad * data_devices
    cols = w_up.shape[2]
    half = cols // 2
    count = tokens.shape[0] // 2
    down_half = w_down.shape[1] // 2

    def pick(if_first, if_second):
        return jnp.where(core == 0, if_first, if_second)

    orders = [links.order(core), links.order(1 - core)]

    def spread_of(order):
        column = jnp.arange(wide)
        place = column % pad
        target = jnp.where(place < own, jnp.repeat(order, pad) * own + place, -1)
        feature = lax.broadcasted_iota(jnp.int32, (feat, wide), 0)
        return (feature == target[None, :]).astype(BF16)

    spreads = [spread_of(order) for order in orders]
    spread_out = pick(spreads[1], spreads[0])
    order_small = pick(orders[0], orders[1])
    device = jnp.arange(data_devices)[:, None]
    to_device = (device == order_small[None, :]).astype(BF16)

    def halves_first(x):
        lead = x.shape[:-1]
        return x.reshape(lead + (data_devices, 2, down_half)).swapaxes(-3, -2).reshape(lead + (cols,))

    def halves_last(x):
        lead = x.shape[:-1]
        return x.reshape(lead + (2, data_devices, down_half)).swapaxes(-3, -2).reshape(lead + (cols,))

    small = jnp.concatenate([norm_gains[0].reshape(-1), biases[0].reshape(-1), up_bias[0]])
    small_size = small.shape[0]
    small = jnp.pad(small, (0, cols - small_size))[None]
    shard_qo = jnp.concatenate([w_qkv[0, :, : 2 * feat], w_out[0], w_qkv[0, :, 2 * feat :]], axis=1)
    shard_qo = jnp.concatenate([shard_qo, small, jnp.zeros((pad - own - 1, cols), BF16)], axis=0)
    shard_up = halves_first(jnp.pad(w_up[0], ((0, pad - own), (0, 0))))
    shard_down = w_down[0]

    def own_halves(shard, size, axis):
        keep = lax.dynamic_slice_in_dim(shard, core * size, size, axis)
        away = lax.dynamic_slice_in_dim(shard, (1 - core) * size, size, axis)
        other = links.swap_cores(away)
        return (pick(keep, other), pick(other, keep))

    halves_qo = own_halves(shard_qo, half, 1)
    halves_up = own_halves(shard_up, half, 1)
    halves_down = own_halves(shard_down, down_half, 0)
    gathers = []
    for layer in range(2):
        gathers.append(Gather(links, halves_qo[layer], False))
        gathers.append(Gather(links, halves_up[layer], False))
        gathers.append(Gather(links, halves_down[layer], True))

    source = lax.dynamic_slice_in_dim(tokens, core * count, count)
    places = lax.dynamic_slice_in_dim(positions, core * count, count)
    cotan = lax.dynamic_slice_in_dim(cotangent, core * count, count)
    states = [{}, {}]

    def forward_attention(layer, rows_in):
        s = states[layer]
        qo = gathers[3 * layer]
        weights = list(qo.live)
        smalls = pick(weights[0], weights[1]).reshape(data_devices, pad, half)[:, own, :small_size]
        smalls = product(to_device, smalls)
        gains = smalls[:, : 2 * own].reshape(data_devices, 2, own)
        gains = gains.transpose(1, 0, 2).reshape(2, feat)
        shifts = smalls[:, 2 * own : 8 * own].reshape(data_devices, 6, own)
        shifts = shifts.transpose(1, 0, 2).reshape(6, feat)
        bias = halves_first(smalls[:, 8 * own :].reshape(-1))
        rows = rows_in.astype(F32)
        normed = norm_rows(rows, gains[0], shifts[0]).astype(BF16)
        normed = [product(normed, spread).astype(BF16) for spread in spreads]
        both = [product(normed[i], weights[i]) for i in range(2)]
        queries = pick(both[0], both[1])
        values = pick(both[1], both[0])[:, feat:]
        joined = jnp.concatenate(
            [queries[:, :feat] + shifts[1], queries[:, feat:], values + shifts[2]], axis=1
        ).astype(BF16)
        mixed, stats = attend(joined, places)
        mixed = product(mixed, spread_out).astype(BF16)
        w_out_all = pick(weights[1], weights[0])[:, :feat]
        hidden = rows + (product(mixed, w_out_all) + shifts[3])
        s.update(
            weights=weights, gains=gains, shifts=shifts, bias=bias, rows=rows, normed_one=normed,
            joined=joined, stats=stats, mixed=mixed, w_out=w_out_all, hidden=hidden,
        )
        return hidden

    def forward_up(layer):
        s = states[layer]
        up = gathers[3 * layer + 1]
        s["up"] = list(up.live)
        normed = norm_rows(s["hidden"], s["gains"][1], s["shifts"][4]).astype(BF16)
        s["normed_two"] = [product(normed, spread).astype(BF16) for spread in spreads]
        bias = s["bias"]
        bias = [pick(bias[:half], bias[half:]), pick(bias[half:], bias[:half])]
        s["inner"] = [product(s["normed_two"][i], s["up"][i]) + bias[i] for i in range(2)]
        s["active"] = [jax.nn.gelu(v, approximate=False).astype(BF16) for v in s["inner"]]
        return s["active"]

    def forward_down(layer):
        s = states[layer]
        down = gathers[3 * layer + 2]
        s["down"] = list(down.live)
        total = sum(product(s["active"][i], s["down"][i]) for i in range(2))
        return (s["hidden"] + (total + s["shifts"][5])).astype(BF16)

    def advance(jobs, slot, stages):
        for back, stage in enumerate(stages):
            if 0 <= slot - back < len(jobs):
                getattr(jobs[slot - back], stage)()

    going = ("stage_turn", "stage_second", "stage_first", "stage_swap")
    def forward_slot(slot, compute, *args):
        advance(gathers, slot, going)
        out = compute(*args) if compute else ()
        if slot >= 8:
            return out
        return fence(gathers, out)

    for slot in range(4):
        forward_slot(slot, None)
    states[0]["hidden"] = forward_slot(4, forward_attention, 0, source)
    states[0]["active"] = forward_slot(5, forward_up, 0)
    first_out = forward_slot(6, forward_down, 0)
    states[1]["hidden"] = forward_slot(7, forward_attention, 1, first_out)
    states[1]["active"] = forward_slot(8, forward_up, 1)
    second_out = forward_down(1)

    def backward_down(layer, grad_rows):
        s = states[layer]
        grads = [outer_sum(s["active"][i], grad_rows).astype(BF16) for i in range(2)]
        s["grad_bdown"] = jnp.sum(grad_rows, axis=0, dtype=F32)
        s["d_inner"] = []
        for i in range(2):
            d_active = against(grad_rows, s["down"][i])
            back = jax.vjp(lambda v: jax.nn.gelu(v, approximate=False), s["inner"][i])[1]
            s["d_inner"].append(back(d_active)[0].astype(BF16))
        return Reduce(links, grads[0], grads[1], True), s["d_inner"]

    def backward_up(layer, grad_rows):
        s = states[layer]
        d_inner = s["d_inner"]
        grads = [outer_sum(s["normed_two"][i], d_inner[i]).astype(BF16) for i in range(2)]
        bups = [jnp.sum(d, axis=0, dtype=F32) for d in d_inner]
        s["grad_bup"] = halves_last(
            jnp.concatenate([pick(bups[0], bups[1]), pick(bups[1], bups[0])])
        )
        d_second = sum(gather_back(against(d_inner[i], s["up"][i]), spreads[i]) for i in range(2))
        back = jax.vjp(norm_rows, s["hidden"], s["gains"][1], s["shifts"][4])[1]
        d_hidden, s["grad_gain_two"], s["grad_shift_two"] = back(d_second)
        d_hidden = grad_rows.astype(F32) + d_hidden
        return Reduce(links, grads[0], grads[1], False), d_hidden

    def backward_attention(layer, d_hidden):
        s = states[layer]
        out_in = d_hidden.astype(BF16)
        d_mixed = against(out_in, s["w_out"]).astype(BF16)
        d_mixed = against(d_mixed, spread_out).astype(BF16)
        return attend_back(s["joined"], places, s["stats"], d_mixed)

    def backward_input(layer, d_hidden, d_joined):
        s = states[layer]
        out_in = d_hidden.astype(BF16)
        grad_bout = jnp.sum(out_in, axis=0, dtype=F32)
        sums = jnp.sum(d_joined, axis=0, dtype=F32)
        d_query, d_key, d_value = (d_joined[:, i * feat : (i + 1) * feat] for i in range(3))
        lone = jnp.zeros_like(d_value)
        kept = jnp.concatenate([d_query, d_key], axis=1)
        rest = jnp.concatenate([lone, d_value], axis=1)
        weights = s["weights"]
        d_first = gather_back(against(pick(kept, rest), weights[0]), spreads[0])
        d_first = d_first + gather_back(against(pick(rest, kept), weights[1]), spreads[1])
        back = jax.vjp(norm_rows, s["rows"], s["gains"][0], s["shifts"][0])[1]
        d_input, grad_gain_one, grad_shift_one = back(d_first)
        d_input = d_hidden + d_input
        small = [
            grad_gain_one, s["grad_gain_two"], grad_shift_one, sums[:feat], sums[2 * feat :],
            grad_bout, s["grad_shift_two"], s["grad_bdown"], s["grad_bup"],
        ]
        small = jnp.concatenate([v.reshape(data_devices, -1) for v in small], axis=1)
        small = outer_sum(to_device, small.astype(BF16)).astype(BF16)
        small = jnp.pad(small, ((0, 0), (0, half - small_size)))
        grads = []
        for i in range(2):
            has_query = core == i
            normed = s["normed_one"][i]
            left = jnp.concatenate([jnp.where(has_query, normed, s["mixed"]), normed], axis=0)
            one = jnp.where(has_query, d_query, out_in)
            two = jnp.where(has_query, d_key, d_value)
            right = jnp.concatenate(
                [jnp.concatenate([one, lone], axis=1), jnp.concatenate([lone, two], axis=1)], axis=0
            )
            grad = outer_sum(left, right).astype(BF16).reshape(data_devices, pad, half)
            row = lax.broadcasted_iota(jnp.int32, grad.shape, 1)
            grad = jnp.where((row == own) & has_query, small[:, None, :], grad)
            grads.append(grad.reshape(wide, half))
        return Reduce(links, grads[0], grads[1], False), d_input

    reduces = []
    returning = ("", "stage_swap", "stage_first", "stage_second", "stage_turn")

    def by_layer(first, second):
        mine = pick(first, second)
        other = links.swap_cores(pick(second, first))
        return pick(mine, other), pick(other, mine)

    begun = []

    def advance_back(slot):
        for job, start in zip(reduces, begun):
            if 1 <= slot - start < 5:
                getattr(job, returning[slot - start])()

    def turn_back(slot, result):
        job, out = result
        if job is not None:
            reduces.append(job)
            begun.append(slot)
        advance_back(slot)
        return fence(reduces, out)

    slot = 0
    grad_in = cotan
    d_inputs = []
    for layer in (1, 0):
        states[layer]["d_inner"] = turn_back(slot, backward_down(layer, grad_in))
        d_hidden = turn_back(slot + 1, backward_up(layer, grad_in))
        d_hidden, d_joined = turn_back(
            slot + 2, (None, (d_hidden, backward_attention(layer, d_hidden)))
        )
        d_input = turn_back(slot + 3, backward_input(layer, d_hidden, d_joined))
        d_inputs.append(d_input)
        grad_in = d_input.astype(BF16)
        slot += 4
    second_grad, first_grad = d_inputs
    for slot in range(8, 12):
        advance_back(slot)
        if slot == 11:
            down_second, up_second, qo_second, down_first, up_first, qo_first = [
                r.live[0] for r in reduces
            ]
            up, down = fence(
                reduces, (by_layer(up_first, up_second), by_layer(down_first, down_second))
            )
            qo_first = reduces[-1].live[0]
        else:
            fence(reduces, ())

    acts = jnp.concatenate(by_layer(first_out, second_out), axis=0)[None]
    grads = jnp.concatenate(by_layer(first_grad, second_grad), axis=0)[None]
    query_key, out_value = [v.reshape(pad, half) for v in by_layer(qo_first, qo_second)]
    up = jnp.concatenate([v.reshape(pad, half) for v in up], axis=1)
    down = jnp.concatenate([v.reshape(down_half, feat) for v in down], axis=0)
    smalls = query_key[own, :small_size]
    return (
        acts,
        grads,
        jnp.concatenate([query_key[:own], out_value[:own, feat:]], axis=1)[None],
        out_value[None, :own, :feat],
        halves_last(up[:own])[None],
        down[None],
        smalls[: 2 * own].reshape(1, 2, own),
        smalls[2 * own : 8 * own].reshape(1, 6, own),
        smalls[8 * own :][None],
    )


def solution(mesh):
    rows = P("dp", None)
    weight = P("section", "dp", None)
    vector = P("section", None, "dp")
    in_specs = (rows, P("dp"), rows, weight, weight, weight, weight, vector, vector, P("section", "dp"))
    out_specs = (weight, weight, weight, weight, weight, weight, vector, vector, P("section", "dp"))
    return jax.shard_map(
        per_device, mesh=mesh, in_specs=in_specs, out_specs=out_specs, check_vma=False
    )
```

```python
import jax
import jax.numpy as jnp
from jax import lax
from jax.sharding import PartitionSpec as P

HEAD_DIM = 64
EPSILON = 1e-05
BOTH = ("section", "dp")
F32 = jnp.float32
BF16 = jnp.bfloat16


def norm_rows(values, gain_row, shift_row):
    row_mean = jnp.mean(values, axis=-1, keepdims=True)
    centred = values - row_mean
    row_var = jnp.mean(centred * centred, axis=-1, keepdims=True)
    return centred * lax.rsqrt(row_var + EPSILON) * gain_row + shift_row


def permitted(places):
    count = places.shape[0]
    query_idx = jnp.arange(count, dtype=jnp.int32)[:, None]
    key_idx = jnp.arange(count, dtype=jnp.int32)[None, :]
    return (key_idx <= query_idx) & (key_idx >= query_idx - places[:, None])


def product(left, right):
    return jnp.dot(left, right, preferred_element_type=F32)


def outer_sum(left, right):
    return lax.dot_general(left, right, (((0,), (0,)), ((), ())), preferred_element_type=F32)


def against(left, right):
    return lax.dot_general(left, right, (((1,), (1,)), ((), ())), preferred_element_type=F32)


class Links:
    def __init__(self, data_devices):
        self.count = data_devices
        self.core = lax.axis_index("section")
        self.me = lax.axis_index("dp")
        self.deep = data_devices // 4
        self.staged = data_devices == 16
        self.quad = self.me % 4
        self.level = self.me // 4
        count = data_devices
        index = [(c, d) for c in range(2) for d in range(count)]

        def pairs(move):
            return [(c * count + d, move(c, d)) for c, d in index]

        self.swap = pairs(lambda c, d: (1 - c) * count + d)
        self.first = pairs(lambda c, d: c * count + (d ^ (2 if c == 0 else 1)))
        self.second = pairs(lambda c, d: c * count + (d ^ (1 if c == 0 else 2)))
        self.levels = {
            k: pairs(lambda c, d, k=k: c * count + (d ^ (4 * k)) % count) for k in (1, 2)
        }

    def by_level(self, x):
        shape = x.shape
        x = x.reshape((2, 2) + shape[1:])
        x = jnp.where(self.level // 2 == 1, x[::-1], x)
        return jnp.where(self.level % 2 == 1, x[:, ::-1], x).reshape(shape)

    def send(self, x, perm):
        return lax.ppermute(x, BOTH, perm)

    def swap_cores(self, x):
        return self.send(x, self.swap)

    def flips(self, core):
        first = jnp.where(core == 0, 2, 1)
        return [0, 3 - first, first, 3]

    def order(self, core):
        if not self.staged:
            return jnp.arange(self.count)
        quads = self.quad ^ jnp.stack([jnp.int32(v) for v in self.flips(core)])
        levels = self.level ^ jnp.arange(self.deep)
        return (levels[None, :] * 4 + quads[:, None]).reshape(-1)


class Gather:
    def __init__(self, links, half, sorted_blocks):
        self.links = links
        self.sorted = sorted_blocks
        self.shape = half.shape
        self.live = [half]

    def stage_turn(self):
        links, (half,) = self.links, self.live
        if not links.staged:
            return
        pair = jnp.stack([half, links.send(half, links.levels[1])])
        turned = jnp.concatenate([pair, links.send(pair, links.levels[2])], axis=0)
        self.live = [links.by_level(turned) if self.sorted else turned]

    def stage_second(self):
        if self.links.staged:
            (mine,) = self.live
            self.live = [jnp.stack([mine, self.links.send(mine, self.links.second)])]

    def stage_first(self):
        links = self.links
        if not links.staged:
            self.live = [lax.all_gather(self.live[0], "dp", axis=0)]
            return
        (pair,) = self.live
        parts = [pair, links.send(pair, links.first)]
        if not self.sorted:
            self.live = [jnp.concatenate(parts, axis=0)]
            return
        out = jnp.zeros((links.deep, 4) + self.shape, pair.dtype)
        for place, flip in enumerate(links.flips(links.core)):
            part = parts[place // 2][place % 2]
            out = lax.dynamic_update_slice_in_dim(out, part[:, None], links.quad ^ flip, 1)
        self.live = [out]

    def stage_swap(self):
        (mine,) = self.live
        mine = mine.reshape(-1, self.shape[1])
        self.live = [mine, self.links.swap_cores(mine)]


class Reduce:
    def __init__(self, links, keep, away, sorted_blocks):
        self.links = links
        self.sorted = sorted_blocks
        shape = (links.count, -1, keep.shape[1])
        self.live = [keep.reshape(shape), away.reshape(shape)]

    def stage_swap(self):
        keep, away = self.live
        total = (keep.astype(F32) + self.links.swap_cores(away).astype(F32)).astype(BF16)
        self.live = [total]

    def stage_first(self):
        links, (total,) = self.links, self.live
        if not links.staged:
            self.live = [lax.psum_scatter(total.astype(F32), "dp", scatter_dimension=0)]
            return
        shape = total.shape[1:]
        if self.sorted:
            quads = total.reshape((links.deep, 4) + shape)
            kept, passed, one, two = [
                lax.dynamic_slice_in_dim(quads, links.quad ^ flip, 1, 1)[:, 0]
                for flip in links.flips(links.core)
            ]
            away = jnp.stack([one, two])
        else:
            quads = total.reshape((4, links.deep) + shape)
            kept, passed, away = quads[0], quads[1], quads[2:]
        arrived = links.send(away, links.first)
        passed = (passed.astype(F32) + arrived[1].astype(F32)).astype(BF16)
        kept = (kept.astype(F32) + arrived[0].astype(F32)).astype(BF16)
        self.live = [kept, passed]

    def stage_second(self):
        if self.links.staged:
            kept, passed = self.live
            arrived = self.links.send(passed, self.links.second)
            self.live = [(kept.astype(F32) + arrived.astype(F32)).astype(BF16)]

    def stage_turn(self):
        links, (kept,) = self.links, self.live
        if links.staged:
            if self.sorted:
                kept = links.by_level(kept)
            arrived = links.send(kept[2:], links.levels[2])
            pair = kept[:2].astype(F32) + arrived.astype(F32)
            result = pair[0] + links.send(pair[1].astype(BF16), links.levels[1]).astype(F32)
            self.live = [result]


def fence(jobs, others):
    held = lax.optimization_barrier(([job.live for job in jobs], others))
    for job, live in zip(jobs, held[0]):
        job.live = live
    return held[1]


def masked_scores(heads_qkv, places):
    scores = jnp.einsum(
        "qhd,khd->hqk", heads_qkv[:, 0], heads_qkv[:, 1], preferred_element_type=F32
    ) * HEAD_DIM ** (-0.5)
    return jnp.where(permitted(places)[None], scores, -jnp.inf)


def attend(joined, places):
    count, wide = joined.shape
    heads_qkv = joined.reshape(count, 3, -1, HEAD_DIM)
    masked = masked_scores(heads_qkv, places)
    row_top = jnp.max(masked, axis=-1, keepdims=True)
    expo_vals = jnp.exp(masked - row_top)
    row_total = jnp.sum(expo_vals, axis=-1, keepdims=True)
    soft_low = (expo_vals / row_total).astype(BF16)
    mixed = jnp.einsum("hqk,khd->qhd", soft_low, heads_qkv[:, 2], preferred_element_type=F32)
    return mixed.reshape(count, wide // 3).astype(BF16), (row_top, row_total)


def attend_back(joined, places, stats, d_mixed):
    count, wide = joined.shape
    row_top, row_total = stats
    heads_qkv = joined.reshape(count, 3, -1, HEAD_DIM)
    d_mixed = d_mixed.reshape(count, -1, HEAD_DIM)
    masked = masked_scores(heads_qkv, places)
    weights_soft = jnp.exp(masked - row_top) / row_total
    soft_low = weights_soft.astype(BF16)
    d_values = jnp.einsum("hqk,qhd->khd", soft_low, d_mixed, preferred_element_type=F32)
    d_soft = jnp.einsum("qhd,khd->hqk", d_mixed, heads_qkv[:, 2], preferred_element_type=F32)
    d_scores = (
        weights_soft * (d_soft - jnp.sum(d_soft * weights_soft, axis=-1, keepdims=True))
    ).astype(BF16)
    scale = HEAD_DIM ** (-0.5)
    d_query = (
        jnp.einsum("hqk,khd->qhd", d_scores, heads_qkv[:, 1], preferred_element_type=F32) * scale
    )
    d_keys = (
        jnp.einsum("hqk,qhd->khd", d_scores, heads_qkv[:, 0], preferred_element_type=F32) * scale
    )
    return jnp.stack([d_query, d_keys, d_values], axis=1).reshape(count, wide).astype(BF16)


def gather_back(values, spread):
    high = lax.reduce_precision(values, 8, 7)
    low = (values - high).astype(BF16)
    return against(high.astype(BF16), spread) + against(low, spread)


def per_device(
    tokens, positions, cotangent, w_qkv, w_out, w_up, w_down, norm_gains, biases, up_bias
):
    data_devices = lax.axis_size("dp")
    links = Links(data_devices)
    core = links.core
    own = w_qkv.shape[1]
    pad = (own // 8 + 1) * 8
    feat = own * data_devices
    wide = pad * data_devices
    cols = w_up.shape[2]
    half = cols // 2
    count = tokens.shape[0] // 2
    down_half = w_down.shape[1] // 2

    def pick(if_first, if_second):
        return jnp.where(core == 0, if_first, if_second)

    orders = [links.order(core), links.order(1 - core)]

    def spread_of(order):
        column = jnp.arange(wide)
        place = column % pad
        target = jnp.where(place < own, jnp.repeat(order, pad) * own + place, -1)
        feature = lax.broadcasted_iota(jnp.int32, (feat, wide), 0)
        return (feature == target[None, :]).astype(BF16)

    spreads = [spread_of(order) for order in orders]
    spread_out = pick(spreads[1], spreads[0])
    order_small = pick(orders[0], orders[1])
    device = jnp.arange(data_devices)[:, None]
    to_device = (device == order_small[None, :]).astype(BF16)

    def halves_first(x):
        lead = x.shape[:-1]
        return x.reshape(lead + (data_devices, 2, down_half)).swapaxes(-3, -2).reshape(lead + (cols,))

    def halves_last(x):
        lead = x.shape[:-1]
        return x.reshape(lead + (2, data_devices, down_half)).swapaxes(-3, -2).reshape(lead + (cols,))

    small = jnp.concatenate([norm_gains[0].reshape(-1), biases[0].reshape(-1), up_bias[0]])
    small_size = small.shape[0]
    small = jnp.pad(small, (0, cols - small_size))[None]
    shard_qo = jnp.concatenate([w_qkv[0, :, : 2 * feat], w_out[0], w_qkv[0, :, 2 * feat :]], axis=1)
    shard_qo = jnp.concatenate([shard_qo, small, jnp.zeros((pad - own - 1, cols), BF16)], axis=0)
    shard_up = halves_first(jnp.pad(w_up[0], ((0, pad - own), (0, 0))))
    shard_down = w_down[0]

    def own_halves(shard, size, axis):
        keep = lax.dynamic_slice_in_dim(shard, core * size, size, axis)
        away = lax.dynamic_slice_in_dim(shard, (1 - core) * size, size, axis)
        other = links.swap_cores(away)
        return (pick(keep, other), pick(other, keep))

    halves_qo = own_halves(shard_qo, half, 1)
    halves_up = own_halves(shard_up, half, 1)
    halves_down = own_halves(shard_down, down_half, 0)
    gathers = []
    for layer in range(2):
        gathers.append(Gather(links, halves_qo[layer], False))
        gathers.append(Gather(links, halves_up[layer], False))
        gathers.append(Gather(links, halves_down[layer], True))

    source = lax.dynamic_slice_in_dim(tokens, core * count, count)
    places = lax.dynamic_slice_in_dim(positions, core * count, count)
    cotan = lax.dynamic_slice_in_dim(cotangent, core * count, count)
    states = [{}, {}]

    def forward_attention(layer, rows_in):
        s = states[layer]
        qo = gathers[3 * layer]
        weights = list(qo.live)
        smalls = pick(weights[0], weights[1]).reshape(data_devices, pad, half)[:, own, :small_size]
        smalls = product(to_device, smalls)
        gains = smalls[:, : 2 * own].reshape(data_devices, 2, own)
        gains = gains.transpose(1, 0, 2).reshape(2, feat)
        shifts = smalls[:, 2 * own : 8 * own].reshape(data_devices, 6, own)
        shifts = shifts.transpose(1, 0, 2).reshape(6, feat)
        bias = halves_first(smalls[:, 8 * own :].reshape(-1))
        rows = rows_in.astype(F32)
        normed = norm_rows(rows, gains[0], shifts[0]).astype(BF16)
        normed = [product(normed, spread).astype(BF16) for spread in spreads]
        both = [product(normed[i], weights[i]) for i in range(2)]
        queries = pick(both[0], both[1])
        values = pick(both[1], both[0])[:, feat:]
        joined = jnp.concatenate(
            [queries[:, :feat] + shifts[1], queries[:, feat:], values + shifts[2]], axis=1
        ).astype(BF16)
        mixed, stats = attend(joined, places)
        mixed = product(mixed, spread_out).astype(BF16)
        w_out_all = pick(weights[1], weights[0])[:, :feat]
        hidden = rows + (product(mixed, w_out_all) + shifts[3])
        s.update(
            weights=weights, gains=gains, shifts=shifts, bias=bias, rows=rows, normed_one=normed,
            joined=joined, stats=stats, mixed=mixed, w_out=w_out_all, hidden=hidden,
        )
        return hidden

    def forward_up(layer):
        s = states[layer]
        up = gathers[3 * layer + 1]
        s["up"] = list(up.live)
        normed = norm_rows(s["hidden"], s["gains"][1], s["shifts"][4]).astype(BF16)
        s["normed_two"] = [product(normed, spread).astype(BF16) for spread in spreads]
        bias = s["bias"]
        bias = [pick(bias[:half], bias[half:]), pick(bias[half:], bias[:half])]
        s["inner"] = [product(s["normed_two"][i], s["up"][i]) + bias[i] for i in range(2)]
        s["active"] = [jax.nn.gelu(v, approximate=False).astype(BF16) for v in s["inner"]]
        return s["active"]

    def forward_down(layer):
        s = states[layer]
        down = gathers[3 * layer + 2]
        s["down"] = list(down.live)
        total = sum(product(s["active"][i], s["down"][i]) for i in range(2))
        return (s["hidden"] + (total + s["shifts"][5])).astype(BF16)

    def advance(jobs, slot, stages):
        for back, stage in reversed(list(enumerate(stages))):
            if 0 <= slot - back < len(jobs):
                getattr(jobs[slot - back], stage)()

    going = ("stage_turn", "stage_second", "stage_first", "stage_swap")
    def forward_slot(slot, compute, *args):
        advance(gathers, slot, going)
        out = compute(*args) if compute else ()
        if slot >= 8:
            return out
        return fence(gathers, out)

    for slot in range(4):
        forward_slot(slot, None)
    states[0]["hidden"] = forward_slot(4, forward_attention, 0, source)
    states[0]["active"] = forward_slot(5, forward_up, 0)
    first_out = forward_slot(6, forward_down, 0)
    states[1]["hidden"] = forward_slot(7, forward_attention, 1, first_out)
    states[1]["active"] = forward_slot(8, forward_up, 1)
    second_out = forward_down(1)

    def backward_down(layer, grad_rows):
        s = states[layer]
        grads = [outer_sum(s["active"][i], grad_rows).astype(BF16) for i in range(2)]
        s["grad_bdown"] = jnp.sum(grad_rows, axis=0, dtype=F32)
        s["d_inner"] = []
        for i in range(2):
            d_active = against(grad_rows, s["down"][i])
            back = jax.vjp(lambda v: jax.nn.gelu(v, approximate=False), s["inner"][i])[1]
            s["d_inner"].append(back(d_active)[0].astype(BF16))
        return Reduce(links, grads[0], grads[1], True), s["d_inner"]

    def backward_up(layer, grad_rows):
        s = states[layer]
        d_inner = s["d_inner"]
        grads = [outer_sum(s["normed_two"][i], d_inner[i]).astype(BF16) for i in range(2)]
        bups = [jnp.sum(d, axis=0, dtype=F32) for d in d_inner]
        s["grad_bup"] = halves_last(
            jnp.concatenate([pick(bups[0], bups[1]), pick(bups[1], bups[0])])
        )
        d_second = sum(gather_back(against(d_inner[i], s["up"][i]), spreads[i]) for i in range(2))
        back = jax.vjp(norm_rows, s["hidden"], s["gains"][1], s["shifts"][4])[1]
        d_hidden, s["grad_gain_two"], s["grad_shift_two"] = back(d_second)
        d_hidden = grad_rows.astype(F32) + d_hidden
        return Reduce(links, grads[0], grads[1], False), d_hidden

    def backward_attention(layer, d_hidden):
        s = states[layer]
        out_in = d_hidden.astype(BF16)
        d_mixed = against(out_in, s["w_out"]).astype(BF16)
        d_mixed = against(d_mixed, spread_out).astype(BF16)
        return attend_back(s["joined"], places, s["stats"], d_mixed)

    def backward_input(layer, d_hidden, d_joined):
        s = states[layer]
        out_in = d_hidden.astype(BF16)
        grad_bout = jnp.sum(out_in, axis=0, dtype=F32)
        sums = jnp.sum(d_joined, axis=0, dtype=F32)
        d_query, d_key, d_value = (d_joined[:, i * feat : (i + 1) * feat] for i in range(3))
        lone = jnp.zeros_like(d_value)
        kept = jnp.concatenate([d_query, d_key], axis=1)
        rest = jnp.concatenate([lone, d_value], axis=1)
        weights = s["weights"]
        d_first = gather_back(against(pick(kept, rest), weights[0]), spreads[0])
        d_first = d_first + gather_back(against(pick(rest, kept), weights[1]), spreads[1])
        back = jax.vjp(norm_rows, s["rows"], s["gains"][0], s["shifts"][0])[1]
        d_input, grad_gain_one, grad_shift_one = back(d_first)
        d_input = d_hidden + d_input
        small = [
            grad_gain_one, s["grad_gain_two"], grad_shift_one, sums[:feat], sums[2 * feat :],
            grad_bout, s["grad_shift_two"], s["grad_bdown"], s["grad_bup"],
        ]
        small = jnp.concatenate([v.reshape(data_devices, -1) for v in small], axis=1)
        small = outer_sum(to_device, small.astype(BF16)).astype(BF16)
        small = jnp.pad(small, ((0, 0), (0, half - small_size)))
        grads = []
        for i in range(2):
            has_query = core == i
            normed = s["normed_one"][i]
            left = jnp.concatenate([jnp.where(has_query, normed, s["mixed"]), normed], axis=0)
            one = jnp.where(has_query, d_query, out_in)
            two = jnp.where(has_query, d_key, d_value)
            right = jnp.concatenate(
                [jnp.concatenate([one, lone], axis=1), jnp.concatenate([lone, two], axis=1)], axis=0
            )
            grad = outer_sum(left, right).astype(BF16).reshape(data_devices, pad, half)
            row = lax.broadcasted_iota(jnp.int32, grad.shape, 1)
            grad = jnp.where((row == own) & has_query, small[:, None, :], grad)
            grads.append(grad.reshape(wide, half))
        return Reduce(links, grads[0], grads[1], False), d_input

    reduces = []
    returning = ("", "stage_swap", "stage_first", "stage_second", "stage_turn")

    def by_layer(first, second):
        mine = pick(first, second)
        other = links.swap_cores(pick(second, first))
        return pick(mine, other), pick(other, mine)

    begun = []

    def advance_back(slot):
        for back in range(1, 5):
            for job, start in zip(reduces, begun):
                if slot - start == back:
                    getattr(job, returning[back])()

    def turn_back(slot, result):
        job, out = result
        if job is not None:
            reduces.append(job)
            begun.append(slot)
        advance_back(slot)
        return fence(reduces, out)

    slot = 0
    grad_in = cotan
    d_inputs = []
    for layer in (1, 0):
        states[layer]["d_inner"] = turn_back(slot, backward_down(layer, grad_in))
        d_hidden = turn_back(slot + 1, backward_up(layer, grad_in))
        d_hidden, d_joined = turn_back(
            slot + 2, (None, (d_hidden, backward_attention(layer, d_hidden)))
        )
        d_input = turn_back(slot + 3, backward_input(layer, d_hidden, d_joined))
        d_inputs.append(d_input)
        grad_in = d_input.astype(BF16)
        slot += 4
    second_grad, first_grad = d_inputs
    for slot in range(8, 12):
        advance_back(slot)
        if slot == 11:
            down_second, up_second, qo_second, down_first, up_first, qo_first = [
                r.live[0] for r in reduces
            ]
            up, down = fence(
                reduces, (by_layer(up_first, up_second), by_layer(down_first, down_second))
            )
            qo_first = reduces[-1].live[0]
        else:
            fence(reduces, ())

    acts = jnp.concatenate(by_layer(first_out, second_out), axis=0)[None]
    grads = jnp.concatenate(by_layer(first_grad, second_grad), axis=0)[None]
    query_key, out_value = [v.reshape(pad, half) for v in by_layer(qo_first, qo_second)]
    up = jnp.concatenate([v.reshape(pad, half) for v in up], axis=1)
    down = jnp.concatenate([v.reshape(down_half, feat) for v in down], axis=0)
    smalls = query_key[own, :small_size]
    return (
        acts,
        grads,
        jnp.concatenate([query_key[:own], out_value[:own, feat:]], axis=1)[None],
        out_value[None, :own, :feat],
        halves_last(up[:own])[None],
        down[None],
        smalls[: 2 * own].reshape(1, 2, own),
        smalls[2 * own : 8 * own].reshape(1, 6, own),
        smalls[8 * own :][None],
    )


def solution(mesh):
    rows = P("dp", None)
    weight = P("section", "dp", None)
    vector = P("section", None, "dp")
    in_specs = (rows, P("dp"), rows, weight, weight, weight, weight, vector, vector, P("section", "dp"))
    out_specs = (weight, weight, weight, weight, weight, weight, vector, vector, P("section", "dp"))
    return jax.shard_map(
        per_device, mesh=mesh, in_specs=in_specs, out_specs=out_specs, check_vma=False
    )
```
